512 devices in a mesh: row: 32 (over z_lo, y, core), col: 16 (over z_hi, x).
Axes of the slice: x: 4, y: 4, z: 16 (z_hi: 4, z_lo: 4; z = z_hi * 4 + z_lo), core: 2. Of those that a mesh axis runs over, the one named last changes fastest.
Arguments:
- iterate: float32 [3584, 14336], P('row', 'col'), may hold values from -0.040089186 to 0.040089186
Outputs:
- update: bfloat16 [3584, 14336], P('row', 'col')
The draws below stay inside these ranges and needn't reach their ends.
All inputs are finite; a program needn't handle non-finite values.
Results may differ from the reference program's by a relative error of at most 0.04.
Values may be sent and summed in bfloat16 or wider, within the bound.
A program may use at most 64 MiB of HBM per device.

```python
import math
import jax
import jax.numpy as jnp
from jax import lax

M = 3584
N = 14336
N_COL = 16


def level_of(rng, shape, cuts, least, high):
    factor_of = 1.0
    for position, blocks in cuts:
        steps = jax.random.uniform(jax.random.fold_in(jax.random.fold_in(rng, 6), position), (blocks,), jnp.float32, least / len(cuts), high / len(cuts))
        factor_of = factor_of * jnp.repeat(jnp.exp(steps), shape[position] // blocks).reshape((-1,) + (1,) * (len(shape) - 1 - position))
    return factor_of


def scatter_about(key, extent, scale, limit, cuts=(), dtype=jnp.bfloat16):
    drawn = scale * jax.random.normal(key, extent, jnp.float32)
    if cuts:
        drawn = drawn * level_of(key, extent, cuts, -0.22, 0.18)
    return jnp.clip(drawn, -limit, limit).astype(dtype)


def setup_inputs(seed: int = 0) -> dict:
    key_list = jax.random.split(jax.random.key(seed), 2)
    return {
        "iterate": scatter_about(key_list[0], (M, N), (0.8 * N ** -0.5), 0.040089186, ((0, 32), (1, 16)), jnp.float32),
    }


def reference(iterate):
    iterate_b = iterate.astype(jnp.bfloat16)
    width = N // N_COL
    gram = jnp.zeros((M, M), jnp.float32)
    for slab_index in range(N_COL):
        slab = iterate_b[:, slab_index * width:(slab_index + 1) * width].astype(jnp.float32)
        partial_gram = jnp.dot(slab, slab.T, precision=lax.Precision.HIGHEST)
        rounded = lax.optimization_barrier(partial_gram.astype(jnp.bfloat16))
        gram = gram + rounded.astype(jnp.float32)
    gram_b = gram.astype(jnp.bfloat16).astype(jnp.float32)
    square = jnp.dot(gram_b, gram_b, precision=lax.Precision.HIGHEST)
    poly = (-4.775 * gram + 2.0315 * square).astype(jnp.bfloat16).astype(jnp.float32)
    product = jnp.dot(poly, iterate_b.astype(jnp.float32), precision=lax.Precision.HIGHEST)
    scale = 0.2 * math.sqrt(N)
    return (scale * (3.4445 * iterate + product)).astype(jnp.bfloat16)
```

```python
import math

import jax
import jax.numpy as jnp
from jax import lax
from jax.experimental import pallas as pl
from jax.experimental.pallas import tpu as pltpu
from jax.sharding import PartitionSpec as P

N = 14336
R = 112
C = 896
W = 256
BF = jnp.bfloat16
F32 = jnp.float32


def dot(a, b):
    return jnp.dot(a, b, preferred_element_type=F32)


def dot_t(a, b):
    return lax.dot_general(a, b, (((1,), (1,)), ((), ())), preferred_element_type=F32)


def rows_of(k):
    return pl.ds(pl.multiple_of(k * R, 16), R)


def cols_of(h):
    return pl.ds(pl.multiple_of(h * W, W), W)


def kernel(
    x_ref, o_ref,
    a_buf, b_buf, gp, rx, zs, rz, gs, gr, gc, pr, ps, osend, ro,
    s_a, r_a, s_b, r_b, s_c, r_c, s_x, r_x, s_z, r_z, s_h, r_h, s_y, r_y,
    s_l, r_l, s_q, r_q, s_k, r_k, s_p, r_p, s_u, r_u, s_o, r_o,
):
    row = lax.axis_index("row")
    col = lax.axis_index("col")
    zl, y, k = row // 8, (row // 2) % 4, row % 2
    zh, x = col // 4, col % 4

    def at(zl=zl, y=y, k=k, zh=zh, x=x):
        return ((zl * 4 + y) * 2 + k, zh * 4 + x)

    def send(src, dst, s, r, device):
        copy = pltpu.make_async_remote_copy(
            src_ref=src, dst_ref=dst, send_sem=s, recv_sem=r,
            device_id=device, device_id_type=pl.DeviceIdType.MESH,
        )
        copy.start()
        sent.append(copy)

    def arrived(ref, s, r):
        pltpu.make_async_remote_copy(
            src_ref=ref, dst_ref=ref, send_sem=s, recv_sem=r,
            device_id=at(k=1 - k), device_id_type=pl.DeviceIdType.MESH,
        ).wait_recv()

    sent = []
    x_b = x_ref[...].astype(BF)
    a_buf[rows_of(y)] = x_b
    b_buf[zl, rows_of(k)] = x_b
    b_buf[:, 2 * R :] = jnp.zeros((4, W - 2 * R, C), BF)
    gc[:, :, 2 * R :] = jnp.zeros((4, 4, W - 2 * R, W), BF)

    barrier = pltpu.get_barrier_semaphore()
    partners = [at(k=1 - k)]
    for d in (1, 2, 3):
        partners += [at(zl=zl ^ d), at(y=y ^ d), at(zh=zh ^ d), at(x=x ^ d)]
    for device in partners:
        pl.semaphore_signal(barrier, inc=1, device_id=device, device_id_type=pl.DeviceIdType.MESH)
    pl.semaphore_wait(barrier, len(partners))

    mine = a_buf.at[rows_of(y)]
    for d in (1, 2, 3):
        to = zl ^ d
        send(mine, b_buf.at[zl, rows_of(k)], s_b.at[d], r_b.at[zl], at(zl=to))
    for d in (1, 3, 2):
        send(mine, mine, s_a.at[d], r_a.at[y], at(y=y ^ d))
    send(mine, b_buf.at[zl, rows_of(k)], s_c.at[0], r_c.at[zl], at(k=1 - k))
    for d in (1, 2, 3):
        f = y ^ d
        arrived(a_buf.at[rows_of(f)], s_a.at[d], r_a.at[f])

    def sum_x(d):
        t = zl ^ d
        total = gp[t, rows_of(x)].astype(F32)
        for e in (1, 2, 3):
            f = x ^ e
            arrived(rx.at[t, f], s_x.at[d, e], r_x.at[t, f])
            total += rx[t, f].astype(F32)
        zs[t] = total.astype(BF)

        @pl.when(t != zh)
        def _():
            copy = pltpu.make_async_remote_copy(
                src_ref=zs.at[t], dst_ref=rz.at[zh], send_sem=s_z.at[t], recv_sem=r_z.at[zh],
                device_id=at(zh=t), device_id_type=pl.DeviceIdType.MESH,
            )
            copy.start()

    for d in range(4):
        t = zl ^ d
        if d:
            arrived(b_buf.at[t, rows_of(k)], s_b.at[d], r_b.at[t])
            send(b_buf.at[t, rows_of(k)], b_buf.at[t, rows_of(k)], s_c.at[d], r_c.at[t], at(k=1 - k))
        arrived(b_buf.at[t, rows_of(1 - k)], s_c.at[d], r_c.at[t])
        gp[t] = dot_t(a_buf[...], b_buf[t]).astype(BF)
        for e in (1, 3, 2):
            to = x ^ e
            send(gp.at[t, rows_of(to)], rx.at[t, x], s_x.at[d, e], r_x.at[t, x], at(x=to))
        if d:
            sum_x(d - 1)
    sum_x(3)

    g = zs[zh].astype(F32)
    for e in (1, 2, 3):
        f = zh ^ e
        arrived(rz.at[f], s_z.at[f], r_z.at[f])
        g += rz[f].astype(F32)
    g_b = g.astype(BF)
    gs[...] = g_b
    gr[y, :, cols_of(zh)] = g_b
    gc[x, zl, rows_of(k)] = g_b
    for e in (1, 2, 3):
        to = zh ^ e
        pltpu.make_async_remote_copy(
            src_ref=zs.at[to], dst_ref=zs.at[to], send_sem=s_z.at[to], recv_sem=r_z.at[to],
            device_id=at(zh=to), device_id_type=pl.DeviceIdType.MESH,
        ).wait_send()

    for e in (1, 2, 3):
        send(gs, gr.at[y, :, cols_of(zh)], s_h.at[e], r_h.at[zh], at(zh=zh ^ e))
        send(gs, gc.at[x, zl, rows_of(k)], s_l.at[e], r_l.at[zl], at(zl=zl ^ e))
    for d in range(4):
        for (f, to_x) in [(zl ^ d, None)]:
            if d:
                arrived(gc.at[x, f, rows_of(k)], s_l.at[d], r_l.at[f])
            part = gc.at[x, f, rows_of(k)]
            for e in (1, 3, 2):
                send(part, part, s_q.at[d, e], r_q.at[x, f], at(x=x ^ e))
            send(part, part, s_k.at[0, d], r_k.at[x, f], at(k=1 - k))
        f = zh ^ d
        if d:
            arrived(gr.at[y, :, cols_of(f)], s_h.at[d], r_h.at[f])
        part = gr.at[y, :, cols_of(f)]
        for e in (1, 3, 2):
            send(part, part, s_y.at[d, e], r_y.at[y, f], at(y=y ^ e))
    for e in (1, 2, 3):
        for d in range(4):
            f, h = x ^ e, zl ^ d
            part = gc.at[f, h, rows_of(k)]
            arrived(part, s_q.at[d, e], r_q.at[f, h])
            send(part, part, s_k.at[e, d], r_k.at[f, h], at(k=1 - k))
    for e in range(4):
        for d in range(4):
            f, h = x ^ e, zl ^ d
            arrived(gc.at[f, h, rows_of(1 - k)], s_k.at[e, d], r_k.at[f, h])
    for e in (1, 2, 3):
        for d in range(4):
            f, h = y ^ e, zh ^ d
            arrived(gr.at[f, :, cols_of(h)], s_y.at[d, e], r_y.at[f, h])
    square = jnp.zeros((R, W), F32)
    for f in range(4):
        square += dot(gr[f], gc[f].reshape(4 * W, W))
    p_b = (-4.775 * g + 2.0315 * square).astype(BF)
    ps[...] = p_b
    pr[x, :, cols_of(zh)] = p_b

    for e in (1, 2, 3):
        send(ps, pr.at[x, :, cols_of(zh)], s_p.at[e], r_p.at[zh], at(zh=zh ^ e))
    for d in range(4):
        f = zh ^ d
        part = pr.at[x, :, cols_of(f)]
        if d:
            arrived(part, s_p.at[d], r_p.at[f])
        for e in (1, 3, 2):
            send(part, part, s_u.at[d, e], r_u.at[x, f], at(x=x ^ e))
    for e in range(4):
        f = x ^ e
        if e:
            for d in range(4):
                h = zh ^ d
                arrived(pr.at[f, :, cols_of(h)], s_u.at[d, e], r_u.at[f, h])
        osend[f] = dot(pr[f], b_buf[...].reshape(4 * W, C)).astype(BF)

        @pl.when(f != y)
        def _():
            pltpu.make_async_remote_copy(
                src_ref=osend.at[f], dst_ref=ro.at[y], send_sem=s_o.at[f], recv_sem=r_o.at[y],
                device_id=at(y=f), device_id_type=pl.DeviceIdType.MESH,
            ).start()

    total = 3.4445 * x_ref[...] + osend[y].astype(F32)
    for e in (1, 2, 3):
        f = y ^ e
        arrived(ro.at[f], s_o.at[f], r_o.at[f])
        total += ro[f].astype(F32)
    o_ref[...] = ((0.2 * math.sqrt(N)) * total).astype(BF)
    for e in (1, 2, 3):
        to = y ^ e
        pltpu.make_async_remote_copy(
            src_ref=osend.at[to], dst_ref=osend.at[to], send_sem=s_o.at[to], recv_sem=r_o.at[to],
            device_id=at(y=to), device_id_type=pl.DeviceIdType.MESH,
        ).wait_send()
    for copy in sent:
        copy.wait_send()


def body(iterate):
    dma = pltpu.SemaphoreType.DMA
    vmem = pl.BlockSpec(memory_space=pltpu.VMEM)
    one, two = dma((4,)), dma((4, 4))
    return pl.pallas_call(
        kernel,
        out_shape=jax.ShapeDtypeStruct((R, C), BF),
        in_specs=[vmem],
        out_specs=vmem,
        scratch_shapes=[
            pltpu.VMEM((4 * R, C), BF),
            pltpu.VMEM((4, W, C), BF),
            pltpu.VMEM((4, 4 * R, W), BF),
            pltpu.VMEM((4, 4, R, W), BF),
            pltpu.VMEM((4, R, W), BF),
            pltpu.VMEM((4, R, W), BF),
            pltpu.VMEM((R, W), BF),
            pltpu.VMEM((4, R, 4 * W), BF),
            pltpu.VMEM((4, 4, W, W), BF),
            pltpu.VMEM((4, R, 4 * W), BF),
            pltpu.VMEM((R, W), BF),
            pltpu.VMEM((4, R, C), BF),
            pltpu.VMEM((4, R, C), BF),
            one, one, one, one, one, one, two, two, one, one, one, one, two, two,
            one, one, two, two, two, two, one, one, two, two, one, one,
        ],
        compiler_params=pltpu.CompilerParams(
            collective_id=0, has_side_effects=True, vmem_limit_bytes=48 * 1024 * 1024
        ),
    )(iterate)


def solution(mesh):
    placed = (P("row", "col"),)
    return jax.shard_map(
        body, mesh=mesh, in_specs=placed, out_specs=P("row", "col"), check_vma=False
    )
```

```python
import math

import jax
import jax.numpy as jnp
from jax import lax
from jax.experimental import pallas as pl
from jax.experimental.pallas import tpu as pltpu
from jax.sharding import PartitionSpec as P

N = 14336
R = 112
C = 896
W = 256
HALF = 64
BF = jnp.bfloat16
F32 = jnp.float32
MESH = pl.DeviceIdType.MESH


def dot(a, b):
    return jnp.dot(a, b, preferred_element_type=F32)


def dot_t(a, b):
    return lax.dot_general(a, b, (((1,), (1,)), ((), ())), preferred_element_type=F32)


def rows_of(k):
    return pl.ds(pl.multiple_of(k * R, 16), R)


def cols_of(h):
    return pl.ds(pl.multiple_of(h * W, W), W)


def kernel(
    x_ref, o_ref,
    a_buf, xs, gp, rx, zs, rz, gs, gr, gc, pz, pr, acc,
    s_all, s_b, s_c, r_a, r_b, r_c, r_x, r_z, r_h, r_hh, r_y, r_l, r_q, r_k, r_p, r_ph, r_u, r_w, r_v,
):
    row = lax.axis_index("row")
    col = lax.axis_index("col")
    zl, y, k = row // 8, (row // 2) % 4, row % 2
    zh, x = col // 4, col % 4
    up, down, far = (zh + 1) % 4, (zh + 3) % 4, (zh + 2) % 4

    def at(zl=zl, y=y, k=k, zh=zh, x=x):
        return ((zl * 4 + y) * 2 + k, zh * 4 + x)

    sent = []

    def copy_of(src, dst, s, r, device):
        return pltpu.make_async_remote_copy(
            src_ref=src, dst_ref=dst, send_sem=s, recv_sem=r, device_id=device, device_id_type=MESH
        )

    def send(src, dst, r, device, when=None):
        copy = copy_of(src, dst, s_all.at[len(sent)], r, device)
        sent.append((copy, when))
        if when is None:
            copy.start()
        else:
            pl.when(when)(copy.start)

    def arrived(ref, r):
        pltpu.make_async_remote_copy(
            src_ref=ref, dst_ref=ref, send_sem=s_all.at[0], recv_sem=r,
            device_id=at(k=1 - k), device_id_type=MESH,
        ).wait_recv()

    barrier = pltpu.get_barrier_semaphore()
    partners = [at(k=1 - k)]
    for d in (1, 2, 3):
        partners += [at(zl=zl ^ d), at(y=y ^ d), at(zh=zh ^ d), at(x=x ^ d)]
    for device in partners:
        pl.semaphore_signal(barrier, inc=1, device_id=device, device_id_type=MESH)
    for f in range(4):

        @pl.when(jnp.logical_or(x != y, y != f))
        def _():
            pl.semaphore_signal(barrier, inc=1, device_id=at(x=y, y=f), device_id_type=MESH)

    x_b = x_ref[...].astype(BF)
    a_buf[rows_of(y)] = x_b
    xs[zl, y, rows_of(k)] = x_b
    xs[:, :, 2 * R :] = jnp.zeros((4, 4, W - 2 * R, C), BF)
    gc[:, :, 2 * R :] = jnp.zeros((4, 4, W - 2 * R, W), BF)
    pl.semaphore_wait(barrier, len(partners) + jnp.where(x == y, 3, 4))

    mine = a_buf.at[rows_of(y)]
    own = xs.at[zl, y, rows_of(k)]
    send(mine, own, r_b.at[zl], at(zl=jnp.minimum(zl + 1, 3)), zl < 3)
    send(mine, own, r_b.at[zl], at(zl=jnp.maximum(zl - 1, 0)), zl > 0)
    send(mine, own, r_c.at[zl], at(k=1 - k))
    for d in (1, 3, 2):
        send(mine, mine, r_a.at[y], at(y=y ^ d))

    def pick(table):
        t = jnp.where(zl == 0, table[0], table[1])
        return jnp.where(zl == 2, table[2], jnp.where(zl == 3, table[3], t))

    order = [zl, pick((1, 0, 1, 2)), pick((2, 2, 3, 1)), pick((3, 3, 0, 0))]
    middle = jnp.logical_and(zl > 0, zl < 3)

    def sum_x(t):
        total = gp[t, rows_of(x)].astype(F32)
        for e in (1, 3, 2):
            f = x ^ e
            arrived(rx.at[t, f], r_x.at[t, f])
            total += rx[t, f].astype(F32)
        zs[t] = total.astype(BF)
        send(zs.at[t], rz.at[zh], r_z.at[zh], at(zh=t), t != zh)

    def pass_on(t):
        part = xs.at[t, y, rows_of(k)]
        arrived(part, r_b.at[t])
        pl.when(middle)(line_copy(t).start)
        core_copy(t).start()

    def line_copy(t):
        part = xs.at[t, y, rows_of(k)]
        to = jnp.clip(jnp.where(t < zl, zl + 1, zl - 1), 0, 3)
        return copy_of(part, part, s_b.at[t], r_b.at[t], at(zl=to))

    def core_copy(t):
        part = xs.at[t, y, rows_of(k)]
        return copy_of(part, part, s_c.at[t], r_c.at[t], at(k=1 - k))

    def partial(t):
        arrived(xs.at[t, y, rows_of(1 - k)], r_c.at[t])
        gp[t] = dot_t(a_buf[...], xs[t, y]).astype(BF)
        for e in (1, 3, 2):
            to = x ^ e
            send(gp.at[t, rows_of(to)], rx.at[t, x], r_x.at[t, x], at(x=to))

    pass_on(order[1])
    pass_on(order[2])
    pl.when(middle)(lambda: pass_on(order[3]))
    for d in (1, 3, 2):
        arrived(a_buf.at[rows_of(y ^ d)], r_a.at[y ^ d])
    partial(order[0])
    partial(order[1])
    for t in order[1:3]:
        part = xs.at[t, y, rows_of(k)]
        for e in (1, 3, 2):
            send(part, part, r_w.at[t, y], at(y=y ^ e))
    sum_x(order[0])
    partial(order[2])
    sum_x(order[1])
    pl.when(jnp.logical_not(middle))(lambda: pass_on(order[3]))
    partial(order[3])
    part = xs.at[order[3], y, rows_of(k)]
    for e in (1, 3, 2):
        send(part, part, r_w.at[order[3], y], at(y=y ^ e))
    sum_x(order[2])
    sum_x(order[3])
    for t in order[1:]:
        pl.when(middle)(line_copy(t).wait_send)
        core_copy(t).wait_send()
        part = xs.at[t, y, rows_of(k)]

    g = zs[zh].astype(F32)
    for f in (up, down, far):
        arrived(rz.at[f], r_z.at[f])
        g += rz[f].astype(F32)
    g_b = g.astype(BF)
    gs[...] = g_b

    def ring(src, slot, r, rh, each, between=lambda: None):
        send(src, slot(zh, 0, R), r.at[zh], at(zh=up))
        send(src, slot(zh, 0, R), r.at[zh], at(zh=down))
        each(zh)
        between()
        arrived(slot(down, 0, R), r.at[down])
        send(slot(down, 0, HALF), slot(down, 0, HALF), rh.at[0], at(zh=up))
        each(down)
        arrived(slot(up, 0, R), r.at[up])
        send(slot(up, HALF, R - HALF), slot(up, HALF, R - HALF), rh.at[1], at(zh=down))
        each(up)

    gr[y, :, cols_of(zh)] = g_b
    gc[x, zl, rows_of(k)] = g_b

    def to_y(f):
        part = gr.at[y, :, cols_of(f)]
        for e in (1, 3, 2):
            send(part, part, r_y.at[y, f], at(y=y ^ e))

    def to_x(f):
        part = gc.at[x, f, rows_of(k)]
        for e in (1, 3, 2):
            send(part, part, r_q.at[x, f], at(x=x ^ e))

    def line():
        for e in (1, 2, 3):
            send(gs, gc.at[x, zl, rows_of(k)], r_l.at[zl], at(zl=zl ^ e))
        to_x(zl)

    def slot(f, start, size):
        return gr.at[y, pl.ds(start, size), cols_of(f)]

    ring(gs, slot, r_h, r_hh, to_y, line)
    for d in (1, 2, 3):
        f = zl ^ d
        arrived(gc.at[x, f, rows_of(k)], r_l.at[f])
        to_x(f)
    part = gc.at[x, :, rows_of(k)]
    send(part, part, r_k.at[x], at(k=1 - k))
    arrived(slot(far, 0, HALF), r_hh.at[0])
    arrived(slot(far, HALF, R - HALF), r_hh.at[1])
    to_y(far)
    for e in (1, 3, 2):
        f = x ^ e
        for h in range(4):
            arrived(gc.at[f, h, rows_of(k)], r_q.at[f, h])
        part = gc.at[f, :, rows_of(k)]
        send(part, part, r_k.at[f], at(k=1 - k))
    square = jnp.zeros((R, W), F32)
    for e in (0, 1, 3, 2):
        f = x ^ e
        arrived(gc.at[f, :, rows_of(1 - k)], r_k.at[f])
    for e in (0, 1, 3, 2):
        f = y ^ e
        if e:
            for h in range(4):
                arrived(gr.at[f, :, cols_of(h)], r_y.at[f, h])
        square += dot(gr[f], gc[f].reshape(4 * W, W))
    p_b = (-4.775 * g + 2.0315 * square).astype(BF)
    pz[zh] = p_b

    def spread(f):
        for e in range(4):
            to = x ^ e
            off = jnp.logical_or(to != x, x != y)
            send(pz.at[f], pr.at[f, :, cols_of(y)], r_u.at[f, y], at(x=to, y=x), off)

        @pl.when(x == y)
        def _():
            pr[f, :, cols_of(y)] = pz[f]

    def other_core():
        for e in (1, 3, 2):
            f = y ^ e
            xs[zl, f, rows_of(k)] = a_buf[rows_of(f)]
        for t in order:
            for e in (1, 3, 2):
                f = y ^ e
                part = xs.at[t, f, rows_of(k)]
                if t is not zl:
                    arrived(part, r_w.at[t, f])
                send(part, part, r_v.at[t, f], at(k=1 - k))

    ring(pz.at[zh], lambda f, start, size: pz.at[f, pl.ds(start, size)], r_p, r_ph, spread, other_core)
    arrived(pz.at[far, pl.ds(0, HALF)], r_ph.at[0])
    arrived(pz.at[far, pl.ds(HALF, R - HALF)], r_ph.at[1])
    spread(far)
    for t in order:
        for e in (1, 3, 2):
            f = y ^ e
            arrived(xs.at[t, f, rows_of(1 - k)], r_v.at[t, f])
    acc[...] = 3.4445 * x_ref[...]
    for f in (zh, down, up, far):
        for e in range(4):
            h = y ^ e

            @pl.when(jnp.logical_or(x != y, h != y))
            def _():
                arrived(pr.at[f, :, cols_of(h)], r_u.at[f, h])

        acc[...] += dot(pr[f], xs[f].reshape(4 * W, C))
    o_ref[...] = ((0.2 * math.sqrt(N)) * acc[...]).astype(BF)
    for copy, when in sent:
        if when is None:
            copy.wait_send()
        else:
            pl.when(when)(copy.wait_send)


def body(iterate):
    dma = pltpu.SemaphoreType.DMA
    vmem = pl.BlockSpec(memory_space=pltpu.VMEM)
    one, two = dma((4,)), dma((4, 4))
    return pl.pallas_call(
        kernel,
        out_shape=jax.ShapeDtypeStruct((R, C), BF),
        in_specs=[vmem],
        out_specs=vmem,
        scratch_shapes=[
            pltpu.VMEM((4 * R, C), BF),
            pltpu.VMEM((4, 4, W, C), BF),
            pltpu.VMEM((4, 4 * R, W), BF),
            pltpu.VMEM((4, 4, R, W), BF),
            pltpu.VMEM((4, R, W), BF),
            pltpu.VMEM((4, R, W), BF),
            pltpu.VMEM((R, W), BF),
            pltpu.VMEM((4, R, 4 * W), BF),
            pltpu.VMEM((4, 4, W, W), BF),
            pltpu.VMEM((4, R, W), BF),
            pltpu.VMEM((4, R, 4 * W), BF),
            pltpu.VMEM((R, C), F32),
            dma((128,)),
            one, one, one, one, one, two, one, one, one, two, one, two, one, one, one, two, two, two,
        ],
        compiler_params=pltpu.CompilerParams(
            collective_id=0, has_side_effects=True, vmem_limit_bytes=48 * 1024 * 1024
        ),
    )(iterate)


def solution(mesh):
    placed = (P("row", "col"),)
    return jax.shard_map(
        body, mesh=mesh, in_specs=placed, out_specs=P("row", "col"), check_vma=False
    )
```

```python
import math

import jax
import jax.numpy as jnp
from jax import lax
from jax.experimental import pallas as pl
from jax.experimental.pallas import tpu as pltpu
from jax.sharding import PartitionSpec as P

N = 14336
R = 112
C = 896
W = 256
HALF = 64
BF = jnp.bfloat16
F32 = jnp.float32
MESH = pl.DeviceIdType.MESH


def dot(a, b):
    return jnp.dot(a, b, preferred_element_type=F32)


def dot_t(a, b):
    return lax.dot_general(a, b, (((1,), (1,)), ((), ())), preferred_element_type=F32)


def rows_of(k):
    return pl.ds(pl.multiple_of(k * R, 16), R)


def cols_of(h):
    return pl.ds(pl.multiple_of(h * W, W), W)


def kernel(
    x_ref, o_ref,
    x_buf, a_buf, xs, gp, rx, zs, rz, gs, gr, gc, pz, pr, acc,
    l_sem, s_all, s_b, s_c, r_a, r_b, r_c, r_x, r_z, r_h, r_hh, r_y, r_l, r_q, r_k, r_p, r_ph, r_u, r_w, r_v,
):
    row = lax.axis_index("row")
    col = lax.axis_index("col")
    zl, y, k = row // 8, (row // 2) % 4, row % 2
    zh, x = col // 4, col % 4
    up, down, far = (zh + 1) % 4, (zh + 3) % 4, (zh + 2) % 4
    y_up, y_down, y_far = (y + 1) % 4, (y + 3) % 4, (y + 2) % 4
    a_rows = (y, y_down, y_up, y_far)

    def at(zl=zl, y=y, k=k, zh=zh, x=x):
        return ((zl * 4 + y) * 2 + k, zh * 4 + x)

    sent = []

    def copy_of(src, dst, s, r, device):
        return pltpu.make_async_remote_copy(
            src_ref=src, dst_ref=dst, send_sem=s, recv_sem=r, device_id=device, device_id_type=MESH
        )

    def send(src, dst, r, device, when=None):
        copy = copy_of(src, dst, s_all.at[len(sent)], r, device)
        sent.append((copy, when))
        if when is None:
            copy.start()
        else:
            pl.when(when)(copy.start)

    def arrived(ref, r):
        pltpu.make_async_remote_copy(
            src_ref=ref, dst_ref=ref, send_sem=s_all.at[0], recv_sem=r,
            device_id=at(k=1 - k), device_id_type=MESH,
        ).wait_recv()

    load = pltpu.make_async_copy(x_ref, x_buf, l_sem)
    load.start()

    barrier = pltpu.get_barrier_semaphore()
    partners = [at(k=1 - k)]
    for d in (1, 2, 3):
        partners += [at(zl=zl ^ d), at(y=y ^ d), at(zh=zh ^ d), at(x=x ^ d)]
    for device in partners:
        pl.semaphore_signal(barrier, inc=1, device_id=device, device_id_type=MESH)
    for f in range(4):

        @pl.when(jnp.logical_or(x != y, y != f))
        def _():
            pl.semaphore_signal(barrier, inc=1, device_id=at(x=y, y=f), device_id_type=MESH)

    load.wait()
    x_b = x_buf[...].astype(BF)
    a_buf[:R] = x_b
    xs[zl, y, rows_of(k)] = x_b
    xs[:, :, 2 * R :] = jnp.zeros((4, 4, W - 2 * R, C), BF)
    gc[:, :, 2 * R :] = jnp.zeros((4, 4, W - 2 * R, W), BF)
    pl.semaphore_wait(barrier, len(partners) + jnp.where(x == y, 3, 4))

    mine = a_buf.at[:R]
    own = xs.at[zl, y, rows_of(k)]
    send(mine, own, r_b.at[zl], at(zl=jnp.minimum(zl + 1, 3)), zl < 3)
    send(mine, own, r_b.at[zl], at(zl=jnp.maximum(zl - 1, 0)), zl > 0)
    send(mine, a_buf.at[pl.ds(R, R)], r_a.at[0], at(y=y_up))
    send(mine, a_buf.at[pl.ds(2 * R, R)], r_a.at[1], at(y=y_down))
    send(mine, own, r_c.at[zl], at(k=1 - k))

    def pick(table, i=zl):
        t = jnp.where(i == 0, table[0], table[1])
        return jnp.where(i == 2, table[2], jnp.where(i == 3, table[3], t))

    order = [zl, pick((1, 0, 1, 2)), pick((2, 2, 3, 1)), pick((3, 3, 0, 0))]
    middle = jnp.logical_and(zl > 0, zl < 3)

    def sum_x(t):
        total = gp[t, rows_of(pick((0, 2, 3, 1), (x + 4 - y) % 4))].astype(F32)
        for e in (1, 3, 2):
            f = x ^ e
            arrived(rx.at[t, f], r_x.at[t, f])
            total += rx[t, f].astype(F32)
        zs[t] = total.astype(BF)
        send(zs.at[t], rz.at[zh], r_z.at[zh], at(zh=t), t != zh)

    def pass_on(t):
        part = xs.at[t, y, rows_of(k)]
        arrived(part, r_b.at[t])
        pl.when(middle)(line_copy(t).start)
        core_copy(t).start()

    def line_copy(t):
        part = xs.at[t, y, rows_of(k)]
        to = jnp.clip(jnp.where(t < zl, zl + 1, zl - 1), 0, 3)
        return copy_of(part, part, s_b.at[t], r_b.at[t], at(zl=to))

    def core_copy(t):
        part = xs.at[t, y, rows_of(k)]
        return copy_of(part, part, s_c.at[t], r_c.at[t], at(k=1 - k))

    def partial(t, parts):
        lo, hi = parts[0], parts[-1] + 1
        gp[t, lo * R : hi * R] = dot_t(a_buf[lo * R : hi * R], xs[t, y]).astype(BF)
        for p in parts:
            to = a_rows[p]
            send(gp.at[t, pl.ds(p * R, R)], rx.at[t, x], r_x.at[t, x], at(x=to), to != x)

    def slab_over_y(t):
        part = xs.at[t, y, rows_of(k)]
        for e in (1, 3, 2):
            send(part, part, r_w.at[t, y], at(y=y ^ e))

    def other_half(t):
        arrived(xs.at[t, y, rows_of(1 - k)], r_c.at[t])

    edge = jnp.logical_not(middle)
    pass_on(order[1])
    pl.when(middle)(lambda: pass_on(order[2]))
    arrived(a_buf.at[pl.ds(R, R)], r_a.at[0])
    send(a_buf.at[pl.ds(R, 64)], a_buf.at[pl.ds(3 * R, 64)], r_a.at[2], at(y=y_up))
    arrived(a_buf.at[pl.ds(2 * R, R)], r_a.at[1])
    send(a_buf.at[pl.ds(2 * R + 64, 48)], a_buf.at[pl.ds(3 * R + 64, 48)], r_a.at[3], at(y=y_down))
    arrived(a_buf.at[pl.ds(3 * R, 64)], r_a.at[2])
    arrived(a_buf.at[pl.ds(3 * R + 64, 48)], r_a.at[3])
    pl.when(edge)(lambda: pass_on(order[2]))
    pl.when(middle)(lambda: pass_on(order[3]))
    for t in order[:3]:
        other_half(t)
        partial(t, (0, 1, 2, 3))
    slab_over_y(order[1])
    slab_over_y(order[2])
    sum_x(order[0])
    pl.when(edge)(lambda: pass_on(order[3]))
    sum_x(order[1])
    other_half(order[3])
    partial(order[3], (0, 1, 2, 3))
    slab_over_y(order[3])
    sum_x(order[2])
    sum_x(order[3])
    for t in order[1:]:
        pl.when(middle)(line_copy(t).wait_send)
        core_copy(t).wait_send()
        part = xs.at[t, y, rows_of(k)]

    g = zs[zh].astype(F32)
    for f in (up, down, far):
        arrived(rz.at[f], r_z.at[f])
        g += rz[f].astype(F32)
    g_b = g.astype(BF)
    gs[...] = g_b

    def ring(src, slot, r, rh, each, between=lambda: None):
        send(src, slot(zh, 0, R), r.at[zh], at(zh=up))
        send(src, slot(zh, 0, R), r.at[zh], at(zh=down))
        each(zh)
        between()
        arrived(slot(down, 0, R), r.at[down])
        send(slot(down, 0, HALF), slot(down, 0, HALF), rh.at[0], at(zh=up))
        each(down)
        arrived(slot(up, 0, R), r.at[up])
        send(slot(up, HALF, R - HALF), slot(up, HALF, R - HALF), rh.at[1], at(zh=down))
        each(up)

    gr[y, :, cols_of(zh)] = g_b
    gc[x, zl, rows_of(k)] = g_b

    def to_y(f):
        part = gr.at[y, :, cols_of(f)]
        for e in (1, 3, 2):
            send(part, part, r_y.at[y, f], at(y=y ^ e))

    def to_x(f):
        part = gc.at[x, f, rows_of(k)]
        for e in (1, 3, 2):
            send(part, part, r_q.at[x, f], at(x=x ^ e))

    def slot(f, start, size):
        return gr.at[y, pl.ds(start, size), cols_of(f)]

    def across(f, h):
        part = gc.at[f, h, rows_of(k)]
        send(part, part, r_k.at[f, h], at(k=1 - k))

    def from_x(h):
        for e in (1, 3, 2):
            arrived(gc.at[x ^ e, h, rows_of(k)], r_q.at[x ^ e, h])
            across(x ^ e, h)

    send(gs, slot(zh, 0, R), r_h.at[zh], at(zh=up))
    send(gs, slot(zh, 0, R), r_h.at[zh], at(zh=down))
    for e in (1, 3, 2):
        send(gs, gc.at[x, zl, rows_of(k)], r_l.at[zl], at(zl=zl ^ e))
    to_x(zl)
    to_y(zh)
    across(x, zl)
    for d in (1, 3, 2):
        f = zl ^ d
        arrived(gc.at[x, f, rows_of(k)], r_l.at[f])
        to_x(f)
        across(x, f)
    arrived(slot(down, 0, R), r_h.at[down])
    send(slot(down, 0, HALF), slot(down, 0, HALF), r_hh.at[0], at(zh=up))
    to_y(down)
    arrived(slot(up, 0, R), r_h.at[up])
    send(slot(up, HALF, R - HALF), slot(up, HALF, R - HALF), r_hh.at[1], at(zh=down))
    to_y(up)
    from_x(zl)
    from_x(zl ^ 1)
    from_x(zl ^ 3)
    arrived(slot(far, 0, HALF), r_hh.at[0])
    arrived(slot(far, HALF, R - HALF), r_hh.at[1])
    to_y(far)
    from_x(zl ^ 2)
    square = jnp.zeros((R, W), F32)
    for e in (0, 1, 3, 2):
        for d in (0, 1, 3, 2):
            arrived(gc.at[x ^ e, zl ^ d, rows_of(1 - k)], r_k.at[x ^ e, zl ^ d])
    for e in (0, 1, 3, 2):
        f = y ^ e
        if e:
            for h in range(4):
                arrived(gr.at[f, :, cols_of(h)], r_y.at[f, h])
        square += dot(gr[f], gc[f].reshape(4 * W, W))
    p_b = (-4.775 * g + 2.0315 * square).astype(BF)
    pz[zh] = p_b

    def spread(f):
        for e in range(4):
            to = x ^ e
            off = jnp.logical_or(to != x, x != y)
            send(pz.at[f], pr.at[f, :, cols_of(y)], r_u.at[f, y], at(x=to, y=x), off)

        @pl.when(x == y)
        def _():
            pr[f, :, cols_of(y)] = pz[f]

    def other_core():
        for p in (1, 2, 3):
            xs[zl, a_rows[p], rows_of(k)] = a_buf[p * R : (p + 1) * R]
        for t in order:
            for e in (1, 3, 2):
                f = y ^ e
                part = xs.at[t, f, rows_of(k)]
                if t is not zl:
                    arrived(part, r_w.at[t, f])
                send(part, part, r_v.at[t, f], at(k=1 - k))

    ring(pz.at[zh], lambda f, start, size: pz.at[f, pl.ds(start, size)], r_p, r_ph, spread)
    other_core()
    arrived(pz.at[far, pl.ds(0, HALF)], r_ph.at[0])
    arrived(pz.at[far, pl.ds(HALF, R - HALF)], r_ph.at[1])
    spread(far)
    for t in order:
        for e in (1, 3, 2):
            f = y ^ e
            arrived(xs.at[t, f, rows_of(1 - k)], r_v.at[t, f])
    acc[...] = 3.4445 * x_buf[...]
    for f in (zh, down, up, far):
        for e in range(4):
            h = y ^ e

            @pl.when(jnp.logical_or(x != y, h != y))
            def _():
                arrived(pr.at[f, :, cols_of(h)], r_u.at[f, h])

        acc[...] += dot(pr[f], xs[f].reshape(4 * W, C))
    o_ref[...] = ((0.2 * math.sqrt(N)) * acc[...]).astype(BF)
    for copy, when in sent:
        if when is None:
            copy.wait_send()
        else:
            pl.when(when)(copy.wait_send)


def body(iterate):
    dma = pltpu.SemaphoreType.DMA
    vmem = pl.BlockSpec(memory_space=pltpu.VMEM)
    one, two = dma((4,)), dma((4, 4))
    return pl.pallas_call(
        kernel,
        out_shape=jax.ShapeDtypeStruct((R, C), BF),
        in_specs=[pl.BlockSpec(memory_space=pl.ANY)],
        out_specs=vmem,
        scratch_shapes=[
            pltpu.VMEM((R, C), F32),
            pltpu.VMEM((4 * R, C), BF),
            pltpu.VMEM((4, 4, W, C), BF),
            pltpu.VMEM((4, 4 * R, W), BF),
            pltpu.VMEM((4, 4, R, W), BF),
            pltpu.VMEM((4, R, W), BF),
            pltpu.VMEM((4, R, W), BF),
            pltpu.VMEM((R, W), BF),
            pltpu.VMEM((4, R, 4 * W), BF),
            pltpu.VMEM((4, 4, W, W), BF),
            pltpu.VMEM((4, R, W), BF),
            pltpu.VMEM((4, R, 4 * W), BF),
            pltpu.VMEM((R, C), F32),
            dma(()),
            dma((128,)),
            one, one, one, one, one, two, one, one, one, two, one, two, two, one, one, two, two, two,
        ],
        compiler_params=pltpu.CompilerParams(
            collective_id=0, has_side_effects=True, vmem_limit_bytes=48 * 1024 * 1024
        ),
    )(iterate)


def solution(mesh):
    placed = (P("row", "col"),)
    return jax.shard_map(
        body, mesh=mesh, in_specs=placed, out_specs=P("row", "col"), check_vma=False
    )
```

```python
import math

import jax
import jax.numpy as jnp
from jax import lax
from jax.experimental import pallas as pl
from jax.experimental.pallas import tpu as pltpu
from jax.sharding import PartitionSpec as P

N = 14336
R = 112
C = 896
W = 256
HALF = 64
BF = jnp.bfloat16
F32 = jnp.float32
MESH = pl.DeviceIdType.MESH


def dot(a, b):
    return jnp.dot(a, b, preferred_element_type=F32)


def dot_t(a, b):
    return lax.dot_general(a, b, (((1,), (1,)), ((), ())), preferred_element_type=F32)


def rows_of(k):
    return pl.ds(pl.multiple_of(k * R, 16), R)


def cols_of(h):
    return pl.ds(pl.multiple_of(h * W, W), W)


def kernel(
    x_ref, o_ref,
    x_buf, a_buf, xs, gp, rx, zs, rz, gs, gr, gc, pz, pr,
    l_sem, s_all, s_b, s_c, r_a, r_b, r_c, r_x, r_z, r_h, r_hh, r_y, r_l, r_q, r_k, r_p, r_ph, r_u, r_w, r_v,
):
    row = lax.axis_index("row")
    col = lax.axis_index("col")
    zl, y, k = row // 8, (row // 2) % 4, row % 2
    zh, x = col // 4, col % 4
    up, down, far = (zh + 1) % 4, (zh + 3) % 4, (zh + 2) % 4
    y_up, y_down, y_far = (y + 1) % 4, (y + 3) % 4, (y + 2) % 4
    a_rows = (y, y_down, y_up, y_far)

    def at(zl=zl, y=y, k=k, zh=zh, x=x):
        return ((zl * 4 + y) * 2 + k, zh * 4 + x)

    sent = []

    def copy_of(src, dst, s, r, device):
        return pltpu.make_async_remote_copy(
            src_ref=src, dst_ref=dst, send_sem=s, recv_sem=r, device_id=device, device_id_type=MESH
        )

    def send(src, dst, r, device, when=None):
        copy = copy_of(src, dst, s_all.at[len(sent)], r, device)
        sent.append((copy, when))
        if when is None:
            copy.start()
        else:
            pl.when(when)(copy.start)

    def arrived(ref, r):
        pltpu.make_async_remote_copy(
            src_ref=ref, dst_ref=ref, send_sem=s_all.at[0], recv_sem=r,
            device_id=at(k=1 - k), device_id_type=MESH,
        ).wait_recv()

    load = pltpu.make_async_copy(x_ref, x_buf, l_sem)
    load.start()

    barrier = pltpu.get_barrier_semaphore()
    partners = [at(k=1 - k)]
    for d in (1, 2, 3):
        partners += [at(zl=zl ^ d), at(y=y ^ d), at(zh=zh ^ d), at(x=x ^ d)]
    for device in partners:
        pl.semaphore_signal(barrier, inc=1, device_id=device, device_id_type=MESH)
    for f in range(4):

        @pl.when(jnp.logical_or(x != y, y != f))
        def _():
            pl.semaphore_signal(barrier, inc=1, device_id=at(x=y, y=f), device_id_type=MESH)

    load.wait()
    x_b = x_buf[...].astype(BF)
    a_buf[:R] = x_b
    xs[zl, y, rows_of(k)] = x_b
    xs[:, :, 2 * R :] = jnp.zeros((4, 4, W - 2 * R, C), BF)
    gc[:, :, 2 * R :] = jnp.zeros((4, 4, W - 2 * R, W), BF)
    pl.semaphore_wait(barrier, len(partners) + jnp.where(x == y, 3, 4))

    mine = a_buf.at[:R]
    own = xs.at[zl, y, rows_of(k)]
    send(mine, own, r_b.at[zl], at(zl=jnp.minimum(zl + 1, 3)), zl < 3)
    send(mine, own, r_b.at[zl], at(zl=jnp.maximum(zl - 1, 0)), zl > 0)
    send(mine, a_buf.at[pl.ds(R, R)], r_a.at[0], at(y=y_up))
    send(mine, a_buf.at[pl.ds(2 * R, R)], r_a.at[1], at(y=y_down))
    send(mine, own, r_c.at[zl], at(k=1 - k))

    def pick(table, i=zl):
        t = jnp.where(i == 0, table[0], table[1])
        return jnp.where(i == 2, table[2], jnp.where(i == 3, table[3], t))

    order = [zl, pick((1, 0, 1, 2)), pick((2, 2, 3, 1)), pick((3, 3, 0, 0))]
    middle = jnp.logical_and(zl > 0, zl < 3)

    def sum_x(t):
        total = gp[t, rows_of(pick((0, 2, 3, 1), (x + 4 - y) % 4))].astype(F32)
        for e in (1, 3, 2):
            f = x ^ e
            arrived(rx.at[t, f], r_x.at[t, f])
            total += rx[t, f].astype(F32)
        zs[t] = total.astype(BF)
        send(zs.at[t], rz.at[zh], r_z.at[zh], at(zh=t), t != zh)

    def pass_on(t):
        part = xs.at[t, y, rows_of(k)]
        arrived(part, r_b.at[t])
        pl.when(middle)(line_copy(t).start)
        core_copy(t).start()

    def line_copy(t):
        part = xs.at[t, y, rows_of(k)]
        to = jnp.clip(jnp.where(t < zl, zl + 1, zl - 1), 0, 3)
        return copy_of(part, part, s_b.at[t], r_b.at[t], at(zl=to))

    def core_copy(t):
        part = xs.at[t, y, rows_of(k)]
        return copy_of(part, part, s_c.at[t], r_c.at[t], at(k=1 - k))

    def partial(t, parts):
        lo, hi = parts[0], parts[-1] + 1
        gp[t, lo * R : hi * R] = dot_t(a_buf[lo * R : hi * R], xs[t, y]).astype(BF)
        for p in parts:
            to = a_rows[p]
            send(gp.at[t, pl.ds(p * R, R)], rx.at[t, x], r_x.at[t, x], at(x=to), to != x)

    def slab_over_y(t):
        part = xs.at[t, y, rows_of(k)]
        for e in (1, 3, 2):
            send(part, part, r_w.at[t, y], at(y=y ^ e))

    def other_half(t):
        arrived(xs.at[t, y, rows_of(1 - k)], r_c.at[t])

    edge = jnp.logical_not(middle)
    pass_on(order[1])
    pl.when(middle)(lambda: pass_on(order[2]))
    arrived(a_buf.at[pl.ds(R, R)], r_a.at[0])
    send(a_buf.at[pl.ds(R, 64)], a_buf.at[pl.ds(3 * R, 64)], r_a.at[2], at(y=y_up))
    arrived(a_buf.at[pl.ds(2 * R, R)], r_a.at[1])
    send(a_buf.at[pl.ds(2 * R + 64, 48)], a_buf.at[pl.ds(3 * R + 64, 48)], r_a.at[3], at(y=y_down))
    arrived(a_buf.at[pl.ds(3 * R, 64)], r_a.at[2])
    arrived(a_buf.at[pl.ds(3 * R + 64, 48)], r_a.at[3])
    pl.when(edge)(lambda: pass_on(order[2]))
    pl.when(middle)(lambda: pass_on(order[3]))
    for t in order[:3]:
        other_half(t)
        partial(t, (0, 1, 2, 3))
    slab_over_y(order[1])
    slab_over_y(order[2])
    sum_x(order[0])
    pl.when(edge)(lambda: pass_on(order[3]))
    sum_x(order[1])
    other_half(order[3])
    partial(order[3], (0, 1, 2, 3))
    slab_over_y(order[3])
    sum_x(order[2])
    sum_x(order[3])
    for t in order[1:]:
        pl.when(middle)(line_copy(t).wait_send)
        core_copy(t).wait_send()
        part = xs.at[t, y, rows_of(k)]

    g = zs[zh].astype(F32)
    for f in (up, down, far):
        arrived(rz.at[f], r_z.at[f])
        g += rz[f].astype(F32)
    g_b = g.astype(BF)
    gs[...] = g_b

    def ring(src, slot, r, rh, each, between=lambda: None):
        send(src, slot(zh, 0, R), r.at[zh], at(zh=up))
        send(src, slot(zh, 0, R), r.at[zh], at(zh=down))
        each(zh)
        between()
        arrived(slot(down, 0, R), r.at[down])
        send(slot(down, 0, HALF), slot(down, 0, HALF), rh.at[0], at(zh=up))
        each(down)
        arrived(slot(up, 0, R), r.at[up])
        send(slot(up, HALF, R - HALF), slot(up, HALF, R - HALF), rh.at[1], at(zh=down))
        each(up)

    gr[y, :, cols_of(zh)] = g_b
    gc[x, zl, rows_of(k)] = g_b

    def to_y(f):
        part = gr.at[y, :, cols_of(f)]
        for e in (1, 3, 2):
            send(part, part, r_y.at[y, f], at(y=y ^ e))

    def to_x(f):
        part = gc.at[x, f, rows_of(k)]
        for e in (1, 3, 2):
            send(part, part, r_q.at[x, f], at(x=x ^ e))

    def slot(f, start, size):
        return gr.at[y, pl.ds(start, size), cols_of(f)]

    def across(f, h):
        part = gc.at[f, h, rows_of(k)]
        send(part, part, r_k.at[f, h], at(k=1 - k))

    def from_x(h):
        for e in (1, 3, 2):
            arrived(gc.at[x ^ e, h, rows_of(k)], r_q.at[x ^ e, h])
            across(x ^ e, h)

    send(gs, slot(zh, 0, R), r_h.at[zh], at(zh=up))
    send(gs, slot(zh, 0, R), r_h.at[zh], at(zh=down))
    for e in (1, 3, 2):
        send(gs, gc.at[x, zl, rows_of(k)], r_l.at[zl], at(zl=zl ^ e))
    to_x(zl)
    to_y(zh)
    across(x, zl)
    for d in (1, 3, 2):
        f = zl ^ d
        arrived(gc.at[x, f, rows_of(k)], r_l.at[f])
        to_x(f)
        across(x, f)
    arrived(slot(down, 0, R), r_h.at[down])
    send(slot(down, 0, HALF), slot(down, 0, HALF), r_hh.at[0], at(zh=up))
    to_y(down)
    arrived(slot(up, 0, R), r_h.at[up])
    send(slot(up, HALF, R - HALF), slot(up, HALF, R - HALF), r_hh.at[1], at(zh=down))
    to_y(up)
    from_x(zl)
    from_x(zl ^ 1)
    from_x(zl ^ 3)
    arrived(slot(far, 0, HALF), r_hh.at[0])
    arrived(slot(far, HALF, R - HALF), r_hh.at[1])
    to_y(far)
    from_x(zl ^ 2)
    square = jnp.zeros((R, W), F32)
    for e in (0, 1, 3, 2):
        for d in (0, 1, 3, 2):
            arrived(gc.at[x ^ e, zl ^ d, rows_of(1 - k)], r_k.at[x ^ e, zl ^ d])
    for e in (0, 1, 3, 2):
        f = y ^ e
        if e:
            for h in range(4):
                arrived(gr.at[f, :, cols_of(h)], r_y.at[f, h])
        square += dot(gr[f], gc[f].reshape(4 * W, W))
    p_b = (-4.775 * g + 2.0315 * square).astype(BF)
    pz[zh] = p_b

    def spread(f):
        for e in range(4):
            to = x ^ e
            off = jnp.logical_or(to != x, x != y)
            send(pz.at[f], pr.at[f, :, cols_of(y)], r_u.at[f, y], at(x=to, y=x), off)

        @pl.when(x == y)
        def _():
            pr[f, :, cols_of(y)] = pz[f]

    def other_core():
        for p in (1, 2, 3):
            xs[zl, a_rows[p], rows_of(k)] = a_buf[p * R : (p + 1) * R]
        for t in order:
            for e in (1, 3, 2):
                f = y ^ e
                part = xs.at[t, f, rows_of(k)]
                if t is not zl:
                    arrived(part, r_w.at[t, f])
                send(part, part, r_v.at[t, f], at(k=1 - k))

    ring(pz.at[zh], lambda f, start, size: pz.at[f, pl.ds(start, size)], r_p, r_ph, spread)
    other_core()
    arrived(pz.at[far, pl.ds(0, HALF)], r_ph.at[0])
    arrived(pz.at[far, pl.ds(HALF, R - HALF)], r_ph.at[1])
    spread(far)
    for t in order:
        for e in (1, 3, 2):
            f = y ^ e
            arrived(xs.at[t, f, rows_of(1 - k)], r_v.at[t, f])
    o_ref[...] = 3.4445 * x_buf[...]
    for f in (zh, down, up, far):
        for e in range(4):
            h = y ^ e

            @pl.when(jnp.logical_or(x != y, h != y))
            def _():
                arrived(pr.at[f, :, cols_of(h)], r_u.at[f, h])

        o_ref[...] += dot(pr[f], xs[f].reshape(4 * W, C))
    for copy, when in sent:
        if when is None:
            copy.wait_send()
        else:
            pl.when(when)(copy.wait_send)


def body(iterate):
    dma = pltpu.SemaphoreType.DMA
    vmem = pl.BlockSpec(memory_space=pltpu.VMEM)
    one, two = dma((4,)), dma((4, 4))
    total = pl.pallas_call(
        kernel,
        out_shape=jax.ShapeDtypeStruct((R, C), F32),
        in_specs=[pl.BlockSpec(memory_space=pl.ANY)],
        out_specs=vmem,
        scratch_shapes=[
            pltpu.VMEM((R, C), F32),
            pltpu.VMEM((4 * R, C), BF),
            pltpu.VMEM((4, 4, W, C), BF),
            pltpu.VMEM((4, 4 * R, W), BF),
            pltpu.VMEM((4, 4, R, W), BF),
            pltpu.VMEM((4, R, W), BF),
            pltpu.VMEM((4, R, W), BF),
            pltpu.VMEM((R, W), BF),
            pltpu.VMEM((4, R, 4 * W), BF),
            pltpu.VMEM((4, 4, W, W), BF),
            pltpu.VMEM((4, R, W), BF),
            pltpu.VMEM((4, R, 4 * W), BF),
            dma(()),
            dma((128,)),
            one, one, one, one, one, two, one, one, one, two, one, two, two, one, one, two, two, two,
        ],
        compiler_params=pltpu.CompilerParams(
            collective_id=0, has_side_effects=True, vmem_limit_bytes=48 * 1024 * 1024
        ),
    )(iterate)
    return ((0.2 * math.sqrt(N)) * total).astype(BF)


def solution(mesh):
    placed = (P("row", "col"),)
    return jax.shard_map(
        body, mesh=mesh, in_specs=placed, out_specs=P("row", "col"), check_vma=False
    )
```

```python
import math

import jax
import jax.numpy as jnp
from jax import lax
from jax.experimental import pallas as pl
from jax.experimental.pallas import tpu as pltpu
from jax.sharding import PartitionSpec as P

N = 14336
R = 112
C = 896
W = 256
BF = jnp.bfloat16
F32 = jnp.float32
MESH = pl.DeviceIdType.MESH


def dot(a, b):
    return jnp.dot(a, b, preferred_element_type=F32)


def dot_t(a, b):
    return lax.dot_general(a, b, (((1,), (1,)), ((), ())), preferred_element_type=F32)


def rows_of(k):
    return pl.ds(pl.multiple_of(k * R, 16), R)


def cols_of(h):
    return pl.ds(pl.multiple_of(h * W, W), W)


def kernel(
    x_ref, o_ref,
    x_buf, a_buf, xs, gp, rx, zs, rz, gs, gr, gc, pz, pr,
    l_sem, s_all, s_b, s_c, r_a, r_b, r_c, r_x, r_z, r_h, r_hh, r_y, r_l, r_q, r_k, r_p, r_ph, r_u, r_w, r_v,
):
    row = lax.axis_index("row")
    col = lax.axis_index("col")
    zl, y, k = row // 8, (row // 2) % 4, row % 2
    zh, x = col // 4, col % 4
    up, down, far = (zh + 1) % 4, (zh + 3) % 4, (zh + 2) % 4
    y_up, y_down, y_far = (y + 1) % 4, (y + 3) % 4, (y + 2) % 4
    a_rows = (y, y_down, y_up, y_far)

    def at(zl=zl, y=y, k=k, zh=zh, x=x):
        return ((zl * 4 + y) * 2 + k, zh * 4 + x)

    sent = []

    def copy_of(src, dst, s, r, device):
        return pltpu.make_async_remote_copy(
            src_ref=src, dst_ref=dst, send_sem=s, recv_sem=r, device_id=device, device_id_type=MESH
        )

    def send(src, dst, r, device, when=None):
        copy = copy_of(src, dst, s_all.at[len(sent)], r, device)
        sent.append((copy, when))
        if when is None:
            copy.start()
        else:
            pl.when(when)(copy.start)

    def arrived(ref, r):
        pltpu.make_async_remote_copy(
            src_ref=ref, dst_ref=ref, send_sem=s_all.at[0], recv_sem=r,
            device_id=at(k=1 - k), device_id_type=MESH,
        ).wait_recv()

    load = pltpu.make_async_copy(x_ref, x_buf, l_sem)
    load.start()

    barrier = pltpu.get_barrier_semaphore()
    partners = [at(k=1 - k)]
    for d in (1, 2, 3):
        partners += [at(zl=zl ^ d), at(y=y ^ d), at(zh=zh ^ d), at(x=x ^ d)]
    for device in partners:
        pl.semaphore_signal(barrier, inc=1, device_id=device, device_id_type=MESH)
    for f in range(4):

        @pl.when(jnp.logical_or(x != y, y != f))
        def _():
            pl.semaphore_signal(barrier, inc=1, device_id=at(x=y, y=f), device_id_type=MESH)

    load.wait()
    x_b = x_buf[...].astype(BF)
    a_buf[:R] = x_b
    xs[zl, y, rows_of(k)] = x_b
    xs[:, :, 2 * R :] = jnp.zeros((4, 4, W - 2 * R, C), BF)
    gc[:, :, 2 * R :] = jnp.zeros((4, 4, W - 2 * R, W), BF)
    pl.semaphore_wait(barrier, len(partners) + jnp.where(x == y, 3, 4))

    mine = a_buf.at[:R]
    own = xs.at[zl, y, rows_of(k)]
    send(mine, own, r_b.at[zl], at(zl=jnp.minimum(zl + 1, 3)), zl < 3)
    send(mine, own, r_b.at[zl], at(zl=jnp.maximum(zl - 1, 0)), zl > 0)
    send(mine, a_buf.at[pl.ds(R, R)], r_a.at[0], at(y=y_up))
    send(mine, a_buf.at[pl.ds(2 * R, R)], r_a.at[1], at(y=y_down))
    send(mine, own, r_c.at[zl], at(k=1 - k))

    def pick(table, i=zl):
        t = jnp.where(i == 0, table[0], table[1])
        return jnp.where(i == 2, table[2], jnp.where(i == 3, table[3], t))

    order = [zl, pick((1, 0, 1, 2)), pick((2, 2, 3, 1)), pick((3, 3, 0, 0))]
    middle = jnp.logical_and(zl > 0, zl < 3)

    def sum_x(t):
        total = gp[t, rows_of(pick((0, 2, 3, 1), (x + 4 - y) % 4))].astype(F32)
        for e in (1, 3, 2):
            f = x ^ e
            arrived(rx.at[t, f], r_x.at[t, f])
            total += rx[t, f].astype(F32)
        zs[t] = total.astype(BF)
        send(zs.at[t], rz.at[zh], r_z.at[zh], at(zh=t), t != zh)

    def pass_on(t):
        part = xs.at[t, y, rows_of(k)]
        arrived(part, r_b.at[t])
        pl.when(middle)(line_copy(t).start)
        core_copy(t).start()

    def line_copy(t):
        part = xs.at[t, y, rows_of(k)]
        to = jnp.clip(jnp.where(t < zl, zl + 1, zl - 1), 0, 3)
        return copy_of(part, part, s_b.at[t], r_b.at[t], at(zl=to))

    def core_copy(t):
        part = xs.at[t, y, rows_of(k)]
        return copy_of(part, part, s_c.at[t], r_c.at[t], at(k=1 - k))

    def partial(t, parts):
        lo, hi = parts[0], parts[-1] + 1
        gp[t, lo * R : hi * R] = dot_t(a_buf[lo * R : hi * R], xs[t, y]).astype(BF)
        for p in parts:
            to = a_rows[p]
            send(gp.at[t, pl.ds(p * R, R)], rx.at[t, x], r_x.at[t, x], at(x=to), to != x)

    def slab_over_y(t):
        part = xs.at[t, y, rows_of(k)]
        for e in (1, 3, 2):
            send(part, part, r_w.at[t, y], at(y=y ^ e))

    def other_half(t):
        arrived(xs.at[t, y, rows_of(1 - k)], r_c.at[t])

    edge = jnp.logical_not(middle)
    pass_on(order[1])
    pl.when(middle)(lambda: pass_on(order[2]))
    arrived(a_buf.at[pl.ds(R, R)], r_a.at[0])
    send(a_buf.at[pl.ds(R, 64)], a_buf.at[pl.ds(3 * R, 64)], r_a.at[2], at(y=y_up))
    arrived(a_buf.at[pl.ds(2 * R, R)], r_a.at[1])
    send(a_buf.at[pl.ds(2 * R + 64, 48)], a_buf.at[pl.ds(3 * R + 64, 48)], r_a.at[3], at(y=y_down))
    arrived(a_buf.at[pl.ds(3 * R, 64)], r_a.at[2])
    arrived(a_buf.at[pl.ds(3 * R + 64, 48)], r_a.at[3])
    pl.when(edge)(lambda: pass_on(order[2]))
    pl.when(middle)(lambda: pass_on(order[3]))
    for t in order[:3]:
        other_half(t)
        partial(t, (0, 1, 2, 3))
    slab_over_y(order[1])
    slab_over_y(order[2])
    sum_x(order[0])
    pl.when(edge)(lambda: pass_on(order[3]))
    sum_x(order[1])
    other_half(order[3])
    partial(order[3], (0, 1, 2, 3))
    slab_over_y(order[3])
    sum_x(order[2])
    sum_x(order[3])
    for t in order[1:]:
        pl.when(middle)(line_copy(t).wait_send)
        core_copy(t).wait_send()
        part = xs.at[t, y, rows_of(k)]

    g = zs[zh].astype(F32)
    for f in (up, down, far):
        arrived(rz.at[f], r_z.at[f])
        g += rz[f].astype(F32)
    g_b = g.astype(BF)
    gs[...] = g_b

    def ring(src, slot, r, rh, each, between=lambda: None):
        send(src, slot(zh, 0, R), r.at[zh], at(zh=up))
        send(src, slot(zh, 0, R), r.at[zh], at(zh=down))
        each(zh)
        between()
        arrived(slot(down, 0, R), r.at[down])
        send(slot(down, 0, R), slot(down, 0, R), rh.at[0], at(zh=up), zl % 2 == 0)
        each(down)
        arrived(slot(up, 0, R), r.at[up])
        send(slot(up, 0, R), slot(up, 0, R), rh.at[0], at(zh=down), zl % 2 == 1)
        each(up)

    gr[y, :, cols_of(zh)] = g_b
    gc[x, zl, rows_of(k)] = g_b

    def to_y(f):
        part = gr.at[y, :, cols_of(f)]
        for e in (1, 3, 2):
            send(part, part, r_y.at[y, f], at(y=y ^ e))

    def to_x(f):
        part = gc.at[x, f, rows_of(k)]
        for e in (1, 3, 2):
            send(part, part, r_q.at[x, f], at(x=x ^ e))

    def slot(f, start, size):
        return gr.at[y, pl.ds(start, size), cols_of(f)]

    def across(f, h):
        part = gc.at[f, h, rows_of(k)]
        send(part, part, r_k.at[f, h], at(k=1 - k))

    def from_x(h):
        for e in (1, 3, 2):
            arrived(gc.at[x ^ e, h, rows_of(k)], r_q.at[x ^ e, h])
            across(x ^ e, h)

    send(gs, slot(zh, 0, R), r_h.at[zh], at(zh=up))
    send(gs, slot(zh, 0, R), r_h.at[zh], at(zh=down))
    for e in (1, 3, 2):
        send(gs, gc.at[x, zl, rows_of(k)], r_l.at[zl], at(zl=zl ^ e))
    to_x(zl)
    to_y(zh)
    across(x, zl)
    for d in (1, 3, 2):
        f = zl ^ d
        arrived(gc.at[x, f, rows_of(k)], r_l.at[f])
        to_x(f)
        across(x, f)
    arrived(slot(down, 0, R), r_h.at[down])
    send(slot(down, 0, R), slot(down, 0, R), r_hh.at[0], at(zh=up), zl % 2 == 0)
    to_y(down)
    arrived(slot(up, 0, R), r_h.at[up])
    send(slot(up, 0, R), slot(up, 0, R), r_hh.at[0], at(zh=down), zl % 2 == 1)
    to_y(up)
    from_x(zl)
    from_x(zl ^ 1)
    from_x(zl ^ 3)
    arrived(slot(far, 0, R), r_hh.at[0])
    to_y(far)
    from_x(zl ^ 2)
    square = jnp.zeros((R, W), F32)
    for e in (0, 1, 3, 2):
        for d in (0, 1, 3, 2):
            arrived(gc.at[x ^ e, zl ^ d, rows_of(1 - k)], r_k.at[x ^ e, zl ^ d])
    for e in (0, 1, 3, 2):
        f = y ^ e
        if e:
            for h in range(4):
                arrived(gr.at[f, :, cols_of(h)], r_y.at[f, h])
        square += dot(gr[f], gc[f].reshape(4 * W, W))
    p_b = (-4.775 * g + 2.0315 * square).astype(BF)
    pz[zh] = p_b

    def spread(f):
        for e in range(4):
            to = x ^ e
            off = jnp.logical_or(to != x, x != y)
            send(pz.at[f], pr.at[f, :, cols_of(y)], r_u.at[f, y], at(x=to, y=x), off)

        @pl.when(x == y)
        def _():
            pr[f, :, cols_of(y)] = pz[f]

    def other_core():
        for p in (1, 2, 3):
            xs[zl, a_rows[p], rows_of(k)] = a_buf[p * R : (p + 1) * R]
        for t in order:
            for e in (1, 3, 2):
                f = y ^ e
                part = xs.at[t, f, rows_of(k)]
                if t is not zl:
                    arrived(part, r_w.at[t, f])
                send(part, part, r_v.at[t, f], at(k=1 - k))

    ring(pz.at[zh], lambda f, start, size: pz.at[f, pl.ds(start, size)], r_p, r_ph, spread)
    other_core()
    arrived(pz.at[far], r_ph.at[0])
    spread(far)
    for t in order:
        for e in (1, 3, 2):
            f = y ^ e
            arrived(xs.at[t, f, rows_of(1 - k)], r_v.at[t, f])
    o_ref[...] = 3.4445 * x_buf[...]
    for f in (zh, down, up, far):
        for e in range(4):
            h = y ^ e

            @pl.when(jnp.logical_or(x != y, h != y))
            def _():
                arrived(pr.at[f, :, cols_of(h)], r_u.at[f, h])

        o_ref[...] += dot(pr[f], xs[f].reshape(4 * W, C))
    for copy, when in sent:
        if when is None:
            copy.wait_send()
        else:
            pl.when(when)(copy.wait_send)


def body(iterate):
    dma = pltpu.SemaphoreType.DMA
    vmem = pl.BlockSpec(memory_space=pltpu.VMEM)
    one, two = dma((4,)), dma((4, 4))
    total = pl.pallas_call(
        kernel,
        out_shape=jax.ShapeDtypeStruct((R, C), F32),
        in_specs=[pl.BlockSpec(memory_space=pl.ANY)],
        out_specs=vmem,
        scratch_shapes=[
            pltpu.VMEM((R, C), F32),
            pltpu.VMEM((4 * R, C), BF),
            pltpu.VMEM((4, 4, W, C), BF),
            pltpu.VMEM((4, 4 * R, W), BF),
            pltpu.VMEM((4, 4, R, W), BF),
            pltpu.VMEM((4, R, W), BF),
            pltpu.VMEM((4, R, W), BF),
            pltpu.VMEM((R, W), BF),
            pltpu.VMEM((4, R, 4 * W), BF),
            pltpu.VMEM((4, 4, W, W), BF),
            pltpu.VMEM((4, R, W), BF),
            pltpu.VMEM((4, R, 4 * W), BF),
            dma(()),
            dma((128,)),
            one, one, one, one, one, two, one, one, one, two, one, two, two, one, one, two, two, two,
        ],
        compiler_params=pltpu.CompilerParams(
            collective_id=0, has_side_effects=True, vmem_limit_bytes=48 * 1024 * 1024
        ),
    )(iterate)
    return ((0.2 * math.sqrt(N)) * total).astype(BF)


def solution(mesh):
    placed = (P("row", "col"),)
    return jax.shard_map(
        body, mesh=mesh, in_specs=placed, out_specs=P("row", "col"), check_vma=False
    )
```
